128 devices in a mesh: dp: 8 (over x, y_hi), expert: 16 (over z, y_lo, core).
Axes of the slice: x: 4, y: 4 (y_hi: 2, y_lo: 2; y = y_hi * 2 + y_lo), z: 4, core: 2. Of those that a mesh axis runs over, the one named last changes fastest.
Arguments:
- tokens: bfloat16 [512, 256, 1280], P(('dp', 'expert')), may hold values from -64 to 64
- router: bfloat16 [1280, 128], replicated, may hold values from -2 to 2
- cotangent: bfloat16 [512, 256, 1280], P(('dp', 'expert')), may hold values from -16 to 16
- slot_out: bfloat16 [512, 128, 1280], P(('dp', 'expert')), may hold values from -6 to 6
- pre_act: bfloat16 [128, 512, 2560], P(('dp', 'expert')), may hold values from -6 to 6
- w_in: bfloat16 [128, 1280, 2560], P(('dp', 'expert')), may hold values from -0.15625 to 0.15625
- w_out: bfloat16 [128, 2560, 1280], P(('dp', 'expert')), may hold values from -0.125 to 0.125
Outputs:
- token_grad: bfloat16 [512, 256, 1280], P(('dp', 'expert'))
- router_grad: float32 [1280, 128], replicated
The draws below stay inside these ranges and needn't reach their ends.
All inputs are finite; a program needn't handle non-finite values.
Results may differ from the reference program's by a relative error of at most 0.012.
Values may be sent and summed in bfloat16 or wider, within the bound.
No kernel may reach another device: no remote copies, remote signals or barrier semaphores. Data moves between devices by JAX's collectives and lax.ppermute only.
A program may use at most 128 MiB of HBM per device.

```python
import math
import jax
import jax.numpy as jnp
from jax import lax

D = 1280
FF = 2560
M = 256
EXPERTS = 128
IMAGES = 512


def shared_directions(key):
    return jax.random.normal(jax.random.fold_in(key, 101), (D, EXPERTS), jnp.float32)


def spread(key, count, lower, upper):
    fraction = jax.random.uniform(key, (count,), jnp.float32)
    return lower * jnp.exp(fraction * math.log(upper / lower))


def draw_router(key, part):
    base = shared_directions(key)
    scale_key = jax.random.fold_in(key, 102)
    scales = spread(scale_key, EXPERTS, 0.3, 3.0)
    return jnp.clip(base * scales[None, :] * D ** (-0.5), -2.0, 2.0).astype(jnp.bfloat16)


def draw_tokens(key, part):
    key = jax.random.fold_in(key, 5)
    first_key, second_key = jax.random.split(key, 2)
    values = jax.random.normal(first_key, (IMAGES, M, D), jnp.float32)
    values = values * spread(second_key, IMAGES * M, 0.3, 3.0).reshape(IMAGES, M, 1)
    return jnp.clip(values, -64.0, 64.0).astype(jnp.bfloat16)


def block_scale(key, extent, cuts, low, high):
    gain, own = 1.0, jax.random.fold_in(key, 6)
    for dim, blocks in cuts:
        steps = jnp.exp(jax.random.uniform(jax.random.fold_in(own, dim), (blocks,), jnp.float32, low / len(cuts), high / len(cuts)))
        gain = gain * jnp.repeat(steps, extent[dim] // blocks).reshape([-1 if axis == dim else 1 for axis in range(len(extent))])
    return gain


def gaussian(rng, dims, scale, limit, cuts=(), dtype=jnp.bfloat16):
    factor_of = block_scale(rng, dims, cuts, -0.22, 0.18) if cuts else 1.0
    entries = jax.random.normal(rng, dims, jnp.float32) * scale * factor_of
    return jnp.minimum(jnp.maximum(entries, -limit), limit).astype(dtype)


def setup_inputs(seed: int = 0) -> dict:
    streams_of = jax.random.split(jax.random.key(seed), 8)
    return {
        "tokens": draw_tokens(jax.random.fold_in(streams_of[7], 71), 0),
        "router": draw_router(jax.random.fold_in(streams_of[7], 71), 0),
        "cotangent": gaussian(streams_of[2], (IMAGES, M, D), 4.0, 16.0, ((0, 128),)),
        "slot_out": gaussian(streams_of[3], (IMAGES, EXPERTS, D), 1.0, 6.0, ((0, 128),)),
        "pre_act": gaussian(streams_of[4], (EXPERTS, IMAGES, FF), 1.0, 6.0, ((0, 128),)),
        "w_in": gaussian(streams_of[5], (EXPERTS, D, FF), D ** -0.5, 0.15625, ((0, 128),)),
        "w_out": gaussian(streams_of[6], (EXPERTS, FF, D), FF ** -0.5, 0.125, ((0, 128),)),
    }


def gelu_slope(values):
    normal_cdf = 0.5 * (1.0 + jax.scipy.special.erf(values * (2.0 ** -0.5)))
    density = jnp.exp(-0.5 * values * values) * ((2.0 * math.pi) ** -0.5)
    return normal_cdf + values * density


def reference(tokens, router, cotangent, slot_out, pre_act, w_in, w_out):
    def front(packed):
        image_tokens, image_cot, image_slots = packed
        logits = jnp.dot(image_tokens, router, preferred_element_type=jnp.float32)
        combine = jax.nn.softmax(logits, axis=1)
        slot_grad = jnp.dot(combine.astype(jnp.bfloat16).T, image_cot, preferred_element_type=jnp.float32).astype(jnp.bfloat16)
        combine_grad = jnp.dot(image_cot, image_slots.T, preferred_element_type=jnp.float32)
        from_combine = combine * (combine_grad - jnp.sum(combine * combine_grad, axis=1, keepdims=True))
        return slot_grad, from_combine

    slot_grads, from_combines = lax.map(front, (tokens, cotangent, slot_out))
    by_expert = jnp.transpose(slot_grads, (1, 0, 2))

    def expert(packed):
        rows, saved, first, second = packed
        hidden_grad = jnp.dot(rows, second.T, preferred_element_type=jnp.float32)
        pre_grad = (hidden_grad * gelu_slope(saved.astype(jnp.float32))).astype(jnp.bfloat16)
        return jnp.dot(pre_grad, first.T, preferred_element_type=jnp.float32).astype(jnp.bfloat16)

    slot_backs = lax.map(expert, (by_expert, pre_act, w_in, w_out))
    returned = jnp.transpose(slot_backs, (1, 0, 2))

    def back(router_sum, packed):
        image_tokens, from_combine, image_back = packed
        logits = jnp.dot(image_tokens, router, preferred_element_type=jnp.float32)
        dispatch = jax.nn.softmax(logits, axis=0)
        dx_dispatch = jnp.dot(dispatch.astype(jnp.bfloat16), image_back, preferred_element_type=jnp.float32)
        dispatch_grad = jnp.dot(image_tokens, image_back.T, preferred_element_type=jnp.float32)
        from_dispatch = dispatch * (dispatch_grad - jnp.sum(dispatch * dispatch_grad, axis=0, keepdims=True))
        logit_grad = (from_combine + from_dispatch).astype(jnp.bfloat16)
        token_grad = (dx_dispatch + jnp.dot(logit_grad, router.T, preferred_element_type=jnp.float32)).astype(jnp.bfloat16)
        router_next = router_sum + jnp.dot(image_tokens.T, logit_grad, preferred_element_type=jnp.float32)
        return router_next, token_grad

    router_sum, token_grads = lax.scan(back, jnp.zeros((D, EXPERTS), jnp.float32), (tokens, from_combines, returned))
    return token_grads, router_sum / IMAGES
```

```python
import functools
import math

import jax
import jax.numpy as jnp
from jax import lax
from jax.experimental import pallas as pl
from jax.experimental.pallas import tpu as pltpu
from jax.sharding import PartitionSpec as P

AXES = ("dp", "expert")
BF = jnp.bfloat16
F32 = jnp.float32
LANES = 128
MIB = 1 << 20


def cost(flops, nbytes, trans=0):
    return pl.CostEstimate(flops=flops, bytes_accessed=nbytes, transcendentals=trans)


def gelu_slope(values):
    normal_cdf = 0.5 * (1.0 + jax.scipy.special.erf(values * 2.0 ** (-0.5)))
    density = jnp.exp(-0.5 * values * values) * (2.0 * math.pi) ** (-0.5)
    return normal_cdf + values * density


def dot(a, b, ca, cb):
    return lax.dot_general(a, b, (((ca,), (cb,)), ((), ())), preferred_element_type=F32)


def softmax(logits, axis):
    e = jnp.exp(logits - jnp.max(logits, axis=axis, keepdims=True))
    return e / jnp.sum(e, axis=axis, keepdims=True)


def front_kernel(tok_ref, router_ref, cot_ref, sg_ref, logits_ref, rows):
    b = pl.program_id(0)
    n = pl.num_programs(0)
    logits = dot(tok_ref[0], router_ref[...], 1, 0)
    logits_ref[0] = logits
    combine = softmax(logits, 1).astype(BF)
    slot_grad = dot(combine, cot_ref[0], 0, 0)
    half_tiles = rows.shape[0]
    experts = slot_grad.shape[0]
    stride = rows.shape[1] // experts
    for t in range(2 * half_tiles):
        h, j = divmod(t, half_tiles)
        rows[j, pl.ds(2 * b + h, experts, stride), :] = slot_grad[:, t * LANES : (t + 1) * LANES]

    @pl.when(b == n - 1)
    def _():
        for j in range(half_tiles):
            sg_ref[:, j * LANES : (j + 1) * LANES] = rows[j].astype(BF)


def front(tokens, router, cotangent):
    images, m, d = tokens.shape
    experts = router.shape[1]
    total = experts * images * 2
    return pl.pallas_call(
        front_kernel,
        grid=(images,),
        in_specs=[
            pl.BlockSpec((1, m, d), lambda b: (b, 0, 0)),
            pl.BlockSpec((d, experts), lambda b: (0, 0)),
            pl.BlockSpec((1, m, d), lambda b: (b, 0, 0)),
        ],
        out_specs=[
            pl.BlockSpec((total, d // 2), lambda b: (0, 0)),
            pl.BlockSpec((1, m, experts), lambda b: (b, 0, 0)),
        ],
        out_shape=[
            jax.ShapeDtypeStruct((total, d // 2), BF),
            jax.ShapeDtypeStruct((images, m, experts), F32),
        ],
        scratch_shapes=[pltpu.VMEM((d // 2 // LANES, total, LANES), F32)],
        compiler_params=pltpu.CompilerParams(vmem_limit_bytes=24 * MIB),
        cost_estimate=cost(4 * images * m * d * experts, 4 * images * m * d + 4 * total * d),
        name="front",
    )(tokens, router, cotangent)


def expert_kernel(x_ref, wo_ref, wi_ref, slope_ref, out_ref, wide, r_ref, pg_ref):
    half_tiles, total, _ = wide.shape
    count = total // 2
    for j in range(half_tiles):
        wide[j] = x_ref[:, j * LANES : (j + 1) * LANES].astype(F32)
    for t in range(2 * half_tiles):
        h, j = divmod(t, half_tiles)
        r_ref[:, t * LANES : (t + 1) * LANES] = wide[j, pl.ds(h, count, 2), :].astype(BF)
    step = 256

    @pl.loop(0, wo_ref.shape[0] // step)
    def _(c):
        cols = pl.ds(pl.multiple_of(c * step, step), step)
        hidden = dot(r_ref[...], wo_ref[cols, :], 1, 1)
        pg_ref[:, cols] = (hidden * slope_ref[:, cols]).astype(BF)

    for c in range(wi_ref.shape[0] // step):
        back = dot(pg_ref[...], wi_ref[c * step : (c + 1) * step, :], 1, 1)
        for u in range(step // LANES):
            h, j = divmod(c * (step // LANES) + u, half_tiles)
            wide[j, pl.ds(h, count, 2), :] = back[:, u * LANES : (u + 1) * LANES]
    for j in range(half_tiles):
        out_ref[:, j * LANES : (j + 1) * LANES] = wide[j].astype(BF)


def expert(x, w_out, w_in, slope):
    total, half = x.shape
    ff, d = w_out.shape
    vmem = pl.BlockSpec(memory_space=pltpu.VMEM)
    return pl.pallas_call(
        expert_kernel,
        in_specs=[vmem] * 4,
        out_specs=vmem,
        out_shape=jax.ShapeDtypeStruct((total, half), BF),
        scratch_shapes=[
            pltpu.VMEM((half // LANES, total, LANES), F32),
            pltpu.VMEM((total // 2, d), BF),
            pltpu.VMEM((total // 2, ff), BF),
        ],
        compiler_params=pltpu.CompilerParams(vmem_limit_bytes=48 * MIB),
        cost_estimate=cost(2 * total * d * ff, 4 * ff * d + 2 * total * ff),
        name="expert",
    )(x, w_out, w_in, slope)


def back(y, tokens, dispatch, from_combine):
    images, m, d = tokens.shape
    experts = dispatch.shape[2]
    total, half = y.shape
    wide_cols = 2 * LANES
    return pl.pallas_call(
        functools.partial(back_kernel, -(-d // LANES // (total // experts))),
        grid=(images,),
        in_specs=[
            pl.BlockSpec((total, half), lambda b: (0, 0)),
            pl.BlockSpec((1, m, d), lambda b: (b, 0, 0)),
            pl.BlockSpec((1, m, experts), lambda b: (b, 0, 0)),
            pl.BlockSpec((1, m, experts), lambda b: (b, 0, 0)),
        ],
        out_specs=[
            pl.BlockSpec((1, m, experts), lambda b: (b, 0, 0)),
            pl.BlockSpec((1, experts, d), lambda b: (b, 0, 0)),
            pl.BlockSpec((total, wide_cols), lambda b: (0, 0)),
        ],
        out_shape=[
            jax.ShapeDtypeStruct((images, m, experts), BF),
            jax.ShapeDtypeStruct((images, experts, d), BF),
            jax.ShapeDtypeStruct((total, wide_cols), BF),
        ],
        scratch_shapes=[
            pltpu.VMEM((half // LANES, total, LANES), F32),
            pltpu.VMEM((experts, d), F32),
        ],
        compiler_params=pltpu.CompilerParams(vmem_limit_bytes=24 * MIB),
        cost_estimate=cost(4 * images * m * d * experts, 4 * images * m * d),
        name="back",
    )(y, tokens, dispatch, from_combine)


def back_kernel(groups, y_ref, tok_ref, disp_ref, fc_ref, lg_ref, sb_ref, term_ref, wide, acc):
    b = pl.program_id(0)
    n = pl.num_programs(0)
    half_tiles, total, _ = wide.shape
    experts = sb_ref.shape[1]
    stride = total // experts

    @pl.when(b == 0)
    def _():
        acc[...] = jnp.zeros_like(acc)
        for j in range(half_tiles):
            wide[j] = y_ref[:, j * LANES : (j + 1) * LANES].astype(F32)

    for t in range(2 * half_tiles):
        h, j = divmod(t, half_tiles)
        sb_ref[0, :, t * LANES : (t + 1) * LANES] = wide[j, pl.ds(2 * b + h, experts, stride), :].astype(BF)
    tok = tok_ref[0]
    disp = disp_ref[0]
    grad = dot(tok, sb_ref[0], 1, 1)
    from_dispatch = disp * (grad - jnp.sum(disp * grad, axis=0, keepdims=True))
    logit_grad = fc_ref[0] + from_dispatch
    lg_ref[0] = logit_grad.astype(BF)
    acc[...] += dot(logit_grad.T.astype(BF), tok, 1, 0)

    @pl.when(b == n - 1)
    def _():
        tiles = acc.shape[1] // LANES
        for t in range(groups * stride):
            part = acc[:, t * LANES : (t + 1) * LANES] if t < tiles else jnp.zeros((experts, LANES), F32)
            j, r = divmod(t, stride)
            wide[j, pl.ds(r, experts, stride), :] = part
        for j in range(groups):
            term_ref[:, j * LANES : (j + 1) * LANES] = wide[j].astype(BF)


def token_kernel(disp_ref, lg_ref, sb_ref, router_t_ref, out_ref):
    left = jnp.concatenate([disp_ref[0].astype(BF), lg_ref[0]], axis=1)
    right = jnp.concatenate([sb_ref[0], router_t_ref[...]], axis=0)
    out_ref[0] = dot(left, right, 1, 0).astype(BF)


def token_side(dispatch, logit_grad, slot_back, router_t):
    images, m, experts = dispatch.shape
    d = router_t.shape[1]
    return pl.pallas_call(
        token_kernel,
        grid=(images,),
        in_specs=[
            pl.BlockSpec((1, m, experts), lambda b: (b, 0, 0)),
            pl.BlockSpec((1, m, experts), lambda b: (b, 0, 0)),
            pl.BlockSpec((1, experts, d), lambda b: (b, 0, 0)),
            pl.BlockSpec((experts, d), lambda b: (0, 0)),
        ],
        out_specs=pl.BlockSpec((1, m, d), lambda b: (b, 0, 0)),
        out_shape=jax.ShapeDtypeStruct((images, m, d), BF),
        compiler_params=pltpu.CompilerParams(vmem_limit_bytes=24 * MIB),
        cost_estimate=cost(4 * images * m * d * experts, 4 * images * m * d),
        name="token_side",
    )(dispatch, logit_grad, slot_back, router_t)


def sum_kernel(scale, x_ref, out_ref):
    devices = out_ref.shape[0]
    total = jnp.sum(x_ref[...].astype(F32), axis=0, keepdims=True) * scale
    out_ref[...] = jnp.broadcast_to(total, out_ref.shape).astype(BF)


def sum_terms(x, scale):
    return pl.pallas_call(
        functools.partial(sum_kernel, scale),
        in_specs=[pl.BlockSpec(memory_space=pltpu.VMEM)],
        out_specs=pl.BlockSpec(memory_space=pltpu.VMEM),
        out_shape=jax.ShapeDtypeStruct(x.shape, BF),
        compiler_params=pltpu.CompilerParams(vmem_limit_bytes=24 * MIB),
        cost_estimate=cost(x.size, 4 * x.size),
        name="sum_terms",
    )(x)


def finish_kernel(x_ref, out_ref, wide):
    groups, total, _ = wide.shape
    experts = out_ref.shape[1]
    stride = total // experts
    for j in range(groups):
        wide[j] = x_ref[:, j * LANES : (j + 1) * LANES].astype(F32)
    for t in range(out_ref.shape[0] // LANES):
        j, r = divmod(t, stride)
        out_ref[t * LANES : (t + 1) * LANES, :] = wide[j, pl.ds(r, experts, stride), :].T


def finish(x, d, experts):
    total, cols = x.shape
    return pl.pallas_call(
        finish_kernel,
        in_specs=[pl.BlockSpec(memory_space=pltpu.VMEM)],
        out_specs=pl.BlockSpec(memory_space=pltpu.VMEM),
        out_shape=jax.ShapeDtypeStruct((d, experts), F32),
        scratch_shapes=[pltpu.VMEM((cols // LANES, total, LANES), F32)],
        compiler_params=pltpu.CompilerParams(vmem_limit_bytes=24 * MIB),
        cost_estimate=cost(x.size, 6 * x.size),
        name="finish",
    )(x)


def exchange(x, devices):
    rows, cols = x.shape
    x = x.reshape(devices, rows // devices, cols)
    return lax.all_to_all(x, AXES, split_axis=0, concat_axis=0, tiled=True).reshape(rows, cols)


def local(tokens, router, cotangent, slot_out, pre_act, w_in, w_out):
    img_dev, m, d = tokens.shape
    experts = router.shape[1]
    devices = lax.axis_size("dp") * lax.axis_size("expert")
    slot_grad, logits = front(tokens, router, cotangent)
    arrived = exchange(slot_grad, devices)

    slope = gelu_slope(pre_act[0].astype(F32))
    combine = jax.nn.softmax(logits, axis=2)
    dispatch = jax.nn.softmax(logits, axis=1)
    combine_grad = jnp.einsum("bmd,bed->bme", cotangent, slot_out, preferred_element_type=F32)
    from_combine = combine * (combine_grad - jnp.sum(combine * combine_grad, axis=2, keepdims=True))

    slot_back = expert(arrived, w_out[0], w_in[0], slope)
    returned = exchange(slot_back, devices)
    logit_grad, slot_back, term = back(returned, tokens, dispatch, from_combine)
    terms = exchange(term, devices)
    token_grad = token_side(dispatch, logit_grad, slot_back, router.T)
    stride = img_dev * 2
    total = sum_terms(terms.reshape(devices, stride, -1), 1.0 / (img_dev * devices))
    gathered = exchange(total.reshape(devices * stride, -1), devices)
    return token_grad, finish(gathered, d, experts)


def solution(mesh):
    spec = P(AXES, None, None)
    return jax.shard_map(
        local,
        mesh=mesh,
        in_specs=(spec, P(), spec, spec, spec, spec, spec),
        out_specs=(spec, P()),
        check_vma=False,
    )
```

```python
import functools
import math

import jax
import jax.numpy as jnp
from jax import lax
from jax.experimental import pallas as pl
from jax.experimental.pallas import tpu as pltpu
from jax.sharding import PartitionSpec as P

AXES = ("dp", "expert")
BF = jnp.bfloat16
F32 = jnp.float32
LANES = 128
MIB = 1 << 20


def cost(flops, nbytes, trans=0):
    return pl.CostEstimate(flops=flops, bytes_accessed=nbytes, transcendentals=trans)


def hbm(x):
    return pltpu.with_memory_space_constraint(x, pltpu.HBM)


def vmem(x):
    return pltpu.with_memory_space_constraint(x, pltpu.VMEM)


WHOLE = pl.BlockSpec(memory_space=pltpu.VMEM)


def gelu_slope(values):
    normal_cdf = 0.5 * (1.0 + jax.scipy.special.erf(values * 2.0 ** (-0.5)))
    density = jnp.exp(-0.5 * values * values) * (2.0 * math.pi) ** (-0.5)
    return normal_cdf + values * density


def dot(a, b, ca, cb):
    return lax.dot_general(a, b, (((ca,), (cb,)), ((), ())), preferred_element_type=F32)


def softmax(logits, axis):
    e = jnp.exp(logits - jnp.max(logits, axis=axis, keepdims=True))
    return e / jnp.sum(e, axis=axis, keepdims=True)


def front_kernel(tok_ref, router_ref, cot_ref, sg_ref, logits_ref, rows):
    b = pl.program_id(0)
    n = pl.num_programs(0)
    logits = dot(tok_ref[0], router_ref[...], 1, 0)
    logits_ref[0] = logits
    combine = softmax(logits, 1).astype(BF)
    slot_grad = dot(combine, cot_ref[0], 0, 0)
    half_tiles = rows.shape[0]
    experts = slot_grad.shape[0]
    stride = rows.shape[1] // experts
    for t in range(2 * half_tiles):
        h, j = divmod(t, half_tiles)
        rows[j, pl.ds(2 * b + h, experts, stride), :] = slot_grad[:, t * LANES : (t + 1) * LANES]

    @pl.when(b == n - 1)
    def _():
        for j in range(half_tiles):
            sg_ref[:, j * LANES : (j + 1) * LANES] = rows[j].astype(BF)


def front(tokens, router, cotangent):
    images, m, d = tokens.shape
    experts = router.shape[1]
    total = experts * images * 2
    return pl.pallas_call(
        front_kernel,
        grid=(images,),
        in_specs=[
            pl.BlockSpec((1, m, d), lambda b: (b, 0, 0)),
            pl.BlockSpec((d, experts), lambda b: (0, 0)),
            pl.BlockSpec((1, m, d), lambda b: (b, 0, 0)),
        ],
        out_specs=[
            pl.BlockSpec((total, d // 2), lambda b: (0, 0)),
            pl.BlockSpec((1, m, experts), lambda b: (b, 0, 0)),
        ],
        out_shape=[
            pltpu.HBM((total, d // 2), BF),
            pltpu.HBM((images, m, experts), F32),
        ],
        scratch_shapes=[pltpu.VMEM((d // 2 // LANES, total, LANES), F32)],
        compiler_params=pltpu.CompilerParams(vmem_limit_bytes=24 * MIB),
        cost_estimate=cost(4 * images * m * d * experts, 4 * images * m * d + 4 * total * d),
        name="front",
    )(hbm(tokens), hbm(router), hbm(cotangent))


STEP_UP = 512
STEP_BACK = 640
WINDOW = 3


def expert_kernel(x_ref, wo_hbm, wi_hbm, slope_hbm, out_hbm, wo, wi, slope, out, wide, rows_ref, pg_ref, w_sems, slope_sems, out_sems):
    half_tiles, total, _ = wide.shape
    count = total // 2
    ff, d = wo.shape
    pieces = [(wo_hbm, wo, pl.ds(c, STEP_UP)) for c in range(0, ff, STEP_UP)]
    ups = len(pieces)
    pieces += [(wi_hbm, wi, pl.ds(c, STEP_BACK)) for c in range(0, d, STEP_BACK)]
    groups = [
        [pltpu.make_async_copy(src.at[r], dst.at[r], w_sems.at[i])] for i, (src, dst, r) in enumerate(pieces)
    ]
    for i in range(ups):
        cols = pl.ds(i * STEP_UP, STEP_UP)
        groups[i].append(pltpu.make_async_copy(slope_hbm.at[:, cols], slope.at[:, cols], slope_sems.at[i]))

    def start(i):
        for copy in groups[i]:
            copy.start()

    def arrive(i):
        for copy in groups[i]:
            copy.wait()
        if i + WINDOW < len(groups):
            start(i + WINDOW)

    for i in range(WINDOW):
        start(i)
    for j in range(half_tiles):
        wide[j] = x_ref[:, j * LANES : (j + 1) * LANES].astype(F32)
    for t in range(2 * half_tiles):
        h, j = divmod(t, half_tiles)
        rows_ref[:, t * LANES : (t + 1) * LANES] = wide[j, pl.ds(h, count, 2), :].astype(BF)
    for i in range(ups):
        arrive(i)
        cols = slice(i * STEP_UP, (i + 1) * STEP_UP)
        hidden = dot(rows_ref[...], wo[cols, :], 1, 1)
        pg_ref[:, cols] = (hidden * slope[:, cols].astype(F32)).astype(BF)
    done, sent = set(), []
    for i in range(d // STEP_BACK):
        arrive(ups + i)
        back = dot(pg_ref[...], wi[i * STEP_BACK : (i + 1) * STEP_BACK, :], 1, 1)
        for u in range(STEP_BACK // LANES):
            t = i * (STEP_BACK // LANES) + u
            h, j = divmod(t, half_tiles)
            wide[j, pl.ds(h, count, 2), :] = back[:, u * LANES : (u + 1) * LANES]
            done.add(t)
            if {j, j + half_tiles} <= done:
                cols = slice(j * LANES, (j + 1) * LANES)
                out[:, cols] = wide[j].astype(BF)
                copy = pltpu.make_async_copy(
                    out.at[:, pl.ds(j * LANES, LANES)], out_hbm.at[:, pl.ds(j * LANES, LANES)], out_sems.at[j]
                )
                copy.start()
                sent.append(copy)
    for copy in sent:
        copy.wait()


def expert(x, w_out, w_in, slope):
    total, half = x.shape
    ff, d = w_out.shape
    raw = pl.BlockSpec(memory_space=pl.ANY)
    return pl.pallas_call(
        expert_kernel,
        in_specs=[WHOLE, raw, raw, raw],
        out_specs=raw,
        out_shape=pltpu.HBM((total, half), BF),
        scratch_shapes=[
            pltpu.VMEM((ff, d), BF),
            pltpu.VMEM((d, ff), BF),
            pltpu.VMEM(slope.shape, slope.dtype),
            pltpu.VMEM((total, half), BF),
            pltpu.VMEM((half // LANES, total, LANES), F32),
            pltpu.VMEM((total // 2, d), BF),
            pltpu.VMEM((total // 2, ff), BF),
            pltpu.SemaphoreType.DMA((ff // STEP_UP + d // STEP_BACK,)),
            pltpu.SemaphoreType.DMA((ff // STEP_UP,)),
            pltpu.SemaphoreType.DMA((half // LANES,)),
        ],
        compiler_params=pltpu.CompilerParams(vmem_limit_bytes=48 * MIB),
        cost_estimate=cost(2 * total * d * ff, 4 * ff * d + 2 * total * ff),
        name="expert",
    )(vmem(x), hbm(w_out), hbm(w_in), hbm(slope))


def back_kernel(
    y_ref, tok_hbm, disp_hbm, fc_hbm, lg_ref, sb_hbm, term_ref, wide, tok_ref, disp_ref, fc_ref, sb_ref, sems, sb_sems
):
    half_tiles, total, _ = wide.shape
    images, experts, d = sb_ref.shape
    stride = total // experts
    pairs = ((tok_hbm, tok_ref), (disp_hbm, disp_ref), (fc_hbm, fc_ref))
    copies = [
        [pltpu.make_async_copy(src.at[b], dst.at[b], sems.at[b, i]) for i, (src, dst) in enumerate(pairs)]
        for b in range(images)
    ]
    sb_copies = [pltpu.make_async_copy(sb_ref.at[b], sb_hbm.at[b], sb_sems.at[b]) for b in range(images)]
    for b in range(images):
        for copy in copies[b]:
            copy.start()
    for j in range(half_tiles):
        wide[j] = y_ref[:, j * LANES : (j + 1) * LANES].astype(F32)
    for b in range(images):
        for t in range(2 * half_tiles):
            h, j = divmod(t, half_tiles)
            sb_ref[b, :, t * LANES : (t + 1) * LANES] = wide[j, pl.ds(2 * b + h, experts, stride), :].astype(BF)
        sb_copies[b].start()
    term = jnp.zeros((experts, d), F32)
    for b in range(images):
        for copy in copies[b]:
            copy.wait()
        tok = tok_ref[b]
        disp = disp_ref[b]
        grad = dot(tok, sb_ref[b], 1, 1)
        from_dispatch = disp * (grad - jnp.sum(disp * grad, axis=0, keepdims=True))
        logit_grad = fc_ref[b] + from_dispatch
        lg_ref[b] = logit_grad.astype(BF)
        term = term + dot(logit_grad.T.astype(BF), tok, 1, 0)
    term_ref[...] = jnp.stack([term[:, : d // 2], term[:, d // 2 :]], axis=1).astype(BF)
    for copy in sb_copies:
        copy.wait()


def back(y, tokens, dispatch, from_combine):
    images, m, d = tokens.shape
    experts = dispatch.shape[2]
    total, half = y.shape
    raw = pl.BlockSpec(memory_space=pl.ANY)
    return pl.pallas_call(
        back_kernel,
        in_specs=[WHOLE, raw, raw, raw],
        out_specs=[WHOLE, raw, WHOLE],
        out_shape=[
            pltpu.VMEM((images, m, experts), BF),
            pltpu.HBM((images, experts, d), BF),
            pltpu.HBM((experts, 2, d // 2), BF),
        ],
        scratch_shapes=[
            pltpu.VMEM((half // LANES, total, LANES), F32),
            pltpu.VMEM((images, m, d), BF),
            pltpu.VMEM((images, m, experts), F32),
            pltpu.VMEM((images, m, experts), F32),
            pltpu.VMEM((images, experts, d), BF),
            pltpu.SemaphoreType.DMA((images, 3)),
            pltpu.SemaphoreType.DMA((images,)),
        ],
        compiler_params=pltpu.CompilerParams(vmem_limit_bytes=32 * MIB),
        cost_estimate=cost(4 * images * m * d * experts, 4 * images * m * d),
        name="back",
    )(vmem(y), hbm(tokens), hbm(dispatch), hbm(from_combine))


def token_kernel(disp_ref, lg_ref, sb_ref, router_t_ref, out_ref):
    b = pl.program_id(0)
    left = jnp.concatenate([disp_ref[0].astype(BF), lg_ref[b]], axis=1)
    right = jnp.concatenate([sb_ref[0], router_t_ref[...]], axis=0)
    out_ref[0] = dot(left, right, 1, 0).astype(BF)


def token_side(dispatch, logit_grad, slot_back, router_t):
    images, m, experts = dispatch.shape
    d = router_t.shape[1]
    return pl.pallas_call(
        token_kernel,
        grid=(images,),
        in_specs=[
            pl.BlockSpec((1, m, experts), lambda b: (b, 0, 0)),
            WHOLE,
            pl.BlockSpec((1, experts, d), lambda b: (b, 0, 0)),
            WHOLE,
        ],
        out_specs=pl.BlockSpec((1, m, d), lambda b: (b, 0, 0)),
        out_shape=pltpu.HBM((images, m, d), BF),
        compiler_params=pltpu.CompilerParams(vmem_limit_bytes=24 * MIB),
        cost_estimate=cost(4 * images * m * d * experts, 4 * images * m * d),
        name="token_side",
    )(hbm(dispatch), vmem(logit_grad), hbm(slot_back), vmem(router_t))


def sum_kernel(scale, x_ref, out_ref):
    devices = out_ref.shape[0]
    total = jnp.sum(x_ref[...].astype(F32), axis=0, keepdims=True) * scale
    out_ref[...] = jnp.broadcast_to(total, out_ref.shape).astype(BF)


def sum_terms(x, scale):
    return pl.pallas_call(
        functools.partial(sum_kernel, scale),
        in_specs=[WHOLE],
        out_specs=WHOLE,
        out_shape=pltpu.HBM(x.shape, BF),
        compiler_params=pltpu.CompilerParams(vmem_limit_bytes=24 * MIB),
        cost_estimate=cost(x.size, 4 * x.size),
        name="sum_terms",
    )(vmem(x))


def finish_kernel(x_ref, out_ref):
    half = x_ref.shape[2]
    wide = x_ref[...].astype(F32)
    for h in range(2):
        part = wide[:, h, :]
        for t in range(half // LANES):
            row = h * half + t * LANES
            out_ref[row : row + LANES, :] = part[:, t * LANES : (t + 1) * LANES].T


def finish(x):
    experts, two, half = x.shape
    return pl.pallas_call(
        finish_kernel,
        in_specs=[WHOLE],
        out_specs=WHOLE,
        out_shape=pltpu.HBM((two * half, experts), F32),
        compiler_params=pltpu.CompilerParams(vmem_limit_bytes=24 * MIB),
        cost_estimate=cost(x.size, 6 * x.size),
        name="finish",
    )(vmem(x))


def exchange(x):
    return lax.all_to_all(x, AXES, split_axis=0, concat_axis=0, tiled=True)


def exchange_rows(x, devices):
    rows, cols = x.shape
    return exchange(x.reshape(devices, rows // devices, cols)).reshape(rows, cols)


def local(tokens, router, cotangent, slot_out, pre_act, w_in, w_out):
    img_dev = tokens.shape[0]
    devices = lax.axis_size("dp") * lax.axis_size("expert")
    slot_grad, logits = front(tokens, router, cotangent)
    arrived = exchange_rows(slot_grad, devices)

    slope = gelu_slope(pre_act[0].astype(F32)).astype(BF)
    combine = jax.nn.softmax(logits, axis=2)
    dispatch = jax.nn.softmax(logits, axis=1)
    combine_grad = jnp.einsum("bmd,bed->bme", cotangent, slot_out, preferred_element_type=F32)
    from_combine = combine * (combine_grad - jnp.sum(combine * combine_grad, axis=2, keepdims=True))

    slot_back = expert(arrived, w_out[0], w_in[0], slope)
    returned = exchange_rows(slot_back, devices)
    logit_grad, slot_back, term = back(returned, tokens, dispatch, from_combine)
    terms = exchange(term)
    token_grad = token_side(dispatch, logit_grad, slot_back, router.T)
    gathered = exchange(sum_terms(terms, 1.0 / (img_dev * devices)))
    return token_grad, finish(gathered)


def solution(mesh):
    spec = P(AXES, None, None)
    return jax.shard_map(
        local,
        mesh=mesh,
        in_specs=(spec, P(), spec, spec, spec, spec, spec),
        out_specs=(spec, P()),
        check_vma=False,
    )
```

```python
import functools
import math

import jax
import jax.numpy as jnp
from jax import lax
from jax.experimental import pallas as pl
from jax.experimental.pallas import tpu as pltpu
from jax.sharding import PartitionSpec as P

AXES = ("dp", "expert")
BF = jnp.bfloat16
F32 = jnp.float32
LANES = 128
MIB = 1 << 20


def cost(flops, nbytes, trans=0):
    return pl.CostEstimate(flops=flops, bytes_accessed=nbytes, transcendentals=trans)


def hbm(x):
    return pltpu.with_memory_space_constraint(x, pltpu.HBM)


def vmem(x):
    return pltpu.with_memory_space_constraint(x, pltpu.VMEM)


WHOLE = pl.BlockSpec(memory_space=pltpu.VMEM)


def gelu_slope(values):
    normal_cdf = 0.5 * (1.0 + jax.scipy.special.erf(values * 2.0 ** (-0.5)))
    density = jnp.exp(-0.5 * values * values) * (2.0 * math.pi) ** (-0.5)
    return normal_cdf + values * density


def dot(a, b, ca, cb):
    return lax.dot_general(a, b, (((ca,), (cb,)), ((), ())), preferred_element_type=F32)


def softmax(logits, axis):
    e = jnp.exp(logits - jnp.max(logits, axis=axis, keepdims=True))
    return e / jnp.sum(e, axis=axis, keepdims=True)


def front_kernel(
    tok_hbm, router_hbm, cot_hbm, sg_hbm, logits_hbm, router, tok, cot, sg, logits_ref, combine, rows, in_sems, l_sem, o_sems
):
    images = tok.shape[0]
    half_tiles, total, _ = rows.shape
    experts = router.shape[1]
    stride = total // experts
    pairs = ((router_hbm, router), (tok_hbm, tok), (cot_hbm, cot))
    router_copy, tok_copy, cot_copy = [
        pltpu.make_async_copy(src, dst, in_sems.at[i]) for i, (src, dst) in enumerate(pairs)
    ]
    for copy in (router_copy, tok_copy, cot_copy):
        copy.start()
    router_copy.wait()
    tok_copy.wait()
    for b in range(images):
        logits = dot(tok[b], router[...], 1, 0)
        logits_ref[b] = logits
        combine[b] = softmax(logits, 1).astype(BF)
    sent = [pltpu.make_async_copy(logits_ref, logits_hbm, l_sem)]
    sent[0].start()
    cot_copy.wait()
    for b in range(images):
        slot_grad = dot(combine[b], cot[b], 0, 0)
        for t in range(2 * half_tiles):
            h, j = divmod(t, half_tiles)
            rows[j, pl.ds(2 * b + h, experts, stride), :] = slot_grad[:, t * LANES : (t + 1) * LANES]
    for j in range(half_tiles):
        sg[:, j * LANES : (j + 1) * LANES] = rows[j].astype(BF)
        cols = pl.ds(j * LANES, LANES)
        sent.append(pltpu.make_async_copy(sg.at[:, cols], sg_hbm.at[:, cols], o_sems.at[j]))
        sent[-1].start()
    for copy in sent:
        copy.wait()


def front(tokens, router, cotangent):
    images, m, d = tokens.shape
    experts = router.shape[1]
    total = experts * images * 2
    half_tiles = d // 2 // LANES
    raw = pl.BlockSpec(memory_space=pl.ANY)
    return pl.pallas_call(
        front_kernel,
        in_specs=[raw] * 3,
        out_specs=[raw] * 2,
        out_shape=[
            pltpu.HBM((total, d // 2), BF),
            pltpu.HBM((images, m, experts), F32),
        ],
        scratch_shapes=[
            pltpu.VMEM(router.shape, BF),
            pltpu.VMEM(tokens.shape, BF),
            pltpu.VMEM(tokens.shape, BF),
            pltpu.VMEM((total, d // 2), BF),
            pltpu.VMEM((images, m, experts), F32),
            pltpu.VMEM((images, m, experts), BF),
            pltpu.VMEM((half_tiles, total, LANES), F32),
            pltpu.SemaphoreType.DMA((3,)),
            pltpu.SemaphoreType.DMA(()),
            pltpu.SemaphoreType.DMA((half_tiles,)),
        ],
        compiler_params=pltpu.CompilerParams(vmem_limit_bytes=32 * MIB),
        cost_estimate=cost(4 * images * m * d * experts, 4 * images * m * d + 4 * total * d),
        name="front",
    )(hbm(tokens), hbm(router), hbm(cotangent))


UP_CUTS = (0, 1024, 2560)
BACK_CUTS = (0, 1280)
WINDOW = 2


def spans(cuts, size):
    return [(lo * size // cuts[-1], hi * size // cuts[-1]) for lo, hi in zip(cuts, cuts[1:])]


def expert_kernel(x_ref, wo_hbm, wi_hbm, slope_hbm, out_hbm, wo, wi, slope, out, wide, rows_ref, pg_ref, w_sems, slope_sems, out_sems):
    half_tiles, total, _ = wide.shape
    count = total // 2
    ff, d = wo.shape
    ups, backs = spans(UP_CUTS, ff), spans(BACK_CUTS, d)
    groups = []
    for i, (lo, hi) in enumerate(ups):
        cut = pl.ds(lo, hi - lo)
        groups.append([
            pltpu.make_async_copy(wo_hbm.at[cut], wo.at[cut], w_sems.at[i]),
            pltpu.make_async_copy(slope_hbm.at[:, cut], slope.at[:, cut], slope_sems.at[i]),
        ])
    for i, (lo, hi) in enumerate(backs):
        cut = pl.ds(lo, hi - lo)
        groups.append([pltpu.make_async_copy(wi_hbm.at[cut], wi.at[cut], w_sems.at[len(ups) + i])])

    def start(i):
        for copy in groups[i]:
            copy.start()

    def arrive(i):
        for copy in groups[i]:
            copy.wait()
        if i + WINDOW < len(groups):
            start(i + WINDOW)

    for i in range(WINDOW):
        start(i)
    for j in range(half_tiles):
        wide[j] = x_ref[:, j * LANES : (j + 1) * LANES].astype(F32)
    for t in range(2 * half_tiles):
        h, j = divmod(t, half_tiles)
        rows_ref[:, t * LANES : (t + 1) * LANES] = wide[j, pl.ds(h, count, 2), :].astype(BF)
    for i, (lo, hi) in enumerate(ups):
        arrive(i)
        hidden = dot(rows_ref[...], wo[lo:hi, :], 1, 1)
        pg_ref[:, lo:hi] = (hidden * slope[:, lo:hi]).astype(BF)
    done, sent = set(), []
    for i, (lo, hi) in enumerate(backs):
        arrive(len(ups) + i)
        back = dot(pg_ref[...], wi[lo:hi, :], 1, 1)
        for t in range(lo // LANES, hi // LANES):
            h, j = divmod(t, half_tiles)
            at = t * LANES - lo
            wide[j, pl.ds(h, count, 2), :] = back[:, at : at + LANES]
            done.add(t)
            if {j, j + half_tiles} <= done:
                cols = slice(j * LANES, (j + 1) * LANES)
                out[:, cols] = wide[j].astype(BF)
                copy = pltpu.make_async_copy(
                    out.at[:, pl.ds(j * LANES, LANES)], out_hbm.at[:, pl.ds(j * LANES, LANES)], out_sems.at[j]
                )
                copy.start()
                sent.append(copy)
    for copy in sent:
        copy.wait()


def expert(x, w_out, w_in, slope):
    total, half = x.shape
    ff, d = w_out.shape
    raw = pl.BlockSpec(memory_space=pl.ANY)
    return pl.pallas_call(
        expert_kernel,
        in_specs=[WHOLE, raw, raw, raw],
        out_specs=raw,
        out_shape=pltpu.HBM((total, half), BF),
        scratch_shapes=[
            pltpu.VMEM((ff, d), BF),
            pltpu.VMEM((d, ff), BF),
            pltpu.VMEM(slope.shape, slope.dtype),
            pltpu.VMEM((total, half), BF),
            pltpu.VMEM((half // LANES, total, LANES), F32),
            pltpu.VMEM((total // 2, d), BF),
            pltpu.VMEM((total // 2, ff), BF),
            pltpu.SemaphoreType.DMA((len(UP_CUTS) + len(BACK_CUTS) - 2,)),
            pltpu.SemaphoreType.DMA((len(UP_CUTS) - 1,)),
            pltpu.SemaphoreType.DMA((half // LANES,)),
        ],
        compiler_params=pltpu.CompilerParams(vmem_limit_bytes=56 * MIB),
        cost_estimate=cost(2 * total * d * ff, 4 * ff * d + 2 * total * ff),
        name="expert",
    )(vmem(x), hbm(w_out), hbm(w_in), hbm(slope))


def back_kernel(
    y_ref, tok_hbm, disp_hbm, fc_hbm, lg_ref, sb_hbm, term_hbm, wide, tok, disp, fc, sb, lg_t, term_ref, in_sems, out_sems
):
    half_tiles, total, _ = wide.shape
    images, experts, d = sb.shape
    m = tok.shape[1]
    stride = total // experts
    pairs = ((tok_hbm, tok), (disp_hbm, disp), (fc_hbm, fc))
    arrivals = [pltpu.make_async_copy(src, dst, in_sems.at[i]) for i, (src, dst) in enumerate(pairs)]
    for copy in arrivals:
        copy.start()
    for j in range(half_tiles):
        wide[j] = y_ref[:, j * LANES : (j + 1) * LANES].astype(F32)
    for b in range(images):
        for t in range(2 * half_tiles):
            h, j = divmod(t, half_tiles)
            sb[b, :, t * LANES : (t + 1) * LANES] = wide[j, pl.ds(2 * b + h, experts, stride), :].astype(BF)
    for copy in arrivals:
        copy.wait()
    for b in range(images):
        grad = dot(tok[b], sb[b], 1, 1)
        from_dispatch = disp[b] * (grad - jnp.sum(disp[b] * grad, axis=0, keepdims=True))
        logit_grad = fc[b] + from_dispatch
        lg_ref[b] = logit_grad.astype(BF)
        lg_t[:, b * m : (b + 1) * m] = logit_grad.T.astype(BF)
    sb_copy = pltpu.make_async_copy(sb, sb_hbm, out_sems.at[0])
    sb_copy.start()
    term = dot(lg_t[...], tok[...].reshape(images * m, d), 1, 0)
    for h in range(2):
        term_ref[:, h, :] = term[:, h * (d // 2) : (h + 1) * (d // 2)].astype(BF)
    term_copy = pltpu.make_async_copy(term_ref, term_hbm, out_sems.at[1])
    term_copy.start()
    sb_copy.wait()
    term_copy.wait()


def back(y, tokens, dispatch, from_combine):
    images, m, d = tokens.shape
    experts = dispatch.shape[2]
    total, half = y.shape
    raw = pl.BlockSpec(memory_space=pl.ANY)
    return pl.pallas_call(
        back_kernel,
        in_specs=[WHOLE, raw, raw, raw],
        out_specs=[WHOLE, raw, raw],
        out_shape=[
            pltpu.VMEM((images, m, experts), BF),
            pltpu.HBM((images, experts, d), BF),
            pltpu.HBM((experts, 2, d // 2), BF),
        ],
        scratch_shapes=[
            pltpu.VMEM((half // LANES, total, LANES), F32),
            pltpu.VMEM((images, m, d), BF),
            pltpu.VMEM((images, m, experts), F32),
            pltpu.VMEM((images, m, experts), F32),
            pltpu.VMEM((images, experts, d), BF),
            pltpu.VMEM((experts, images * m), BF),
            pltpu.VMEM((experts, 2, d // 2), BF),
            pltpu.SemaphoreType.DMA((3,)),
            pltpu.SemaphoreType.DMA((2,)),
        ],
        compiler_params=pltpu.CompilerParams(vmem_limit_bytes=32 * MIB),
        cost_estimate=cost(4 * images * m * d * experts, 4 * images * m * d),
        name="back",
    )(vmem(y), hbm(tokens), hbm(dispatch), hbm(from_combine))


def token_kernel(disp_ref, lg_ref, sb_ref, router_t_ref, out_ref):
    b = pl.program_id(0)
    left = jnp.concatenate([disp_ref[0].astype(BF), lg_ref[b]], axis=1)
    right = jnp.concatenate([sb_ref[0], router_t_ref[...]], axis=0)
    out_ref[0] = dot(left, right, 1, 0).astype(BF)


def token_side(dispatch, logit_grad, slot_back, router_t):
    images, m, experts = dispatch.shape
    d = router_t.shape[1]
    return pl.pallas_call(
        token_kernel,
        grid=(images,),
        in_specs=[
            pl.BlockSpec((1, m, experts), lambda b: (b, 0, 0)),
            WHOLE,
            pl.BlockSpec((1, experts, d), lambda b: (b, 0, 0)),
            WHOLE,
        ],
        out_specs=pl.BlockSpec((1, m, d), lambda b: (b, 0, 0)),
        out_shape=pltpu.HBM((images, m, d), BF),
        compiler_params=pltpu.CompilerParams(vmem_limit_bytes=24 * MIB),
        cost_estimate=cost(4 * images * m * d * experts, 4 * images * m * d),
        name="token_side",
    )(hbm(dispatch), vmem(logit_grad), hbm(slot_back), vmem(router_t))


def sum_kernel(scale, x_ref, out_ref):
    step = 8
    part = x_ref[:step].astype(F32)
    for i in range(step, x_ref.shape[0], step):
        part = part + x_ref[i : i + step].astype(F32)
    total = jnp.sum(part, axis=0, keepdims=True) * scale
    out_ref[...] = jnp.broadcast_to(total.astype(BF), out_ref.shape)


def sum_terms(x, scale):
    return pl.pallas_call(
        functools.partial(sum_kernel, scale),
        in_specs=[WHOLE],
        out_specs=WHOLE,
        out_shape=pltpu.HBM(x.shape, BF),
        compiler_params=pltpu.CompilerParams(vmem_limit_bytes=24 * MIB),
        cost_estimate=cost(x.size, 4 * x.size),
        name="sum_terms",
    )(vmem(x))


def finish_kernel(x_ref, out_ref):
    half = x_ref.shape[2]
    wide = x_ref[...].astype(F32)
    for h in range(2):
        part = wide[:, h, :]
        for t in range(half // LANES):
            row = h * half + t * LANES
            out_ref[row : row + LANES, :] = part[:, t * LANES : (t + 1) * LANES].T


def finish(x):
    experts, two, half = x.shape
    return pl.pallas_call(
        finish_kernel,
        in_specs=[WHOLE],
        out_specs=WHOLE,
        out_shape=pltpu.HBM((two * half, experts), F32),
        compiler_params=pltpu.CompilerParams(vmem_limit_bytes=24 * MIB),
        cost_estimate=cost(x.size, 6 * x.size),
        name="finish",
    )(vmem(x))


def exchange(x):
    return lax.all_to_all(x, AXES, split_axis=0, concat_axis=0, tiled=True)


def exchange_rows(x, devices):
    rows, cols = x.shape
    return exchange(x.reshape(devices, rows // devices, cols)).reshape(rows, cols)


def local(tokens, router, cotangent, slot_out, pre_act, w_in, w_out):
    img_dev = tokens.shape[0]
    devices = lax.axis_size("dp") * lax.axis_size("expert")
    slot_grad, logits = front(tokens, router, cotangent)
    arrived = exchange_rows(slot_grad, devices)

    slope = gelu_slope(pre_act[0].astype(F32))
    combine = jax.nn.softmax(logits, axis=2)
    dispatch = jax.nn.softmax(logits, axis=1)
    combine_grad = jnp.einsum("bmd,bed->bme", cotangent, slot_out, preferred_element_type=F32)
    from_combine = combine * (combine_grad - jnp.sum(combine * combine_grad, axis=2, keepdims=True))

    slot_back = expert(arrived, w_out[0], w_in[0], slope)
    returned = exchange_rows(slot_back, devices)
    logit_grad, slot_back, term = back(returned, tokens, dispatch, from_combine)
    terms = exchange(term)
    token_grad = token_side(dispatch, logit_grad, slot_back, router.T)
    gathered = exchange(sum_terms(terms, 1.0 / (img_dev * devices)))
    return token_grad, finish(gathered)


def solution(mesh):
    spec = P(AXES, None, None)
    return jax.shard_map(
        local,
        mesh=mesh,
        in_specs=(spec, P(), spec, spec, spec, spec, spec),
        out_specs=(spec, P()),
        check_vma=False,
    )
```

```python
import functools
import math

import jax
import jax.numpy as jnp
from jax import lax
from jax.experimental import pallas as pl
from jax.experimental.pallas import tpu as pltpu
from jax.sharding import PartitionSpec as P

AXES = ("dp", "expert")
BF = jnp.bfloat16
F32 = jnp.float32
LANES = 128
MIB = 1 << 20


def cost(flops, nbytes, trans=0):
    return pl.CostEstimate(flops=flops, bytes_accessed=nbytes, transcendentals=trans)


def hbm(x):
    return pltpu.with_memory_space_constraint(x, pltpu.HBM)


def vmem(x):
    return pltpu.with_memory_space_constraint(x, pltpu.VMEM)


WHOLE = pl.BlockSpec(memory_space=pltpu.VMEM)


def gelu_slope(values):
    normal_cdf = 0.5 * (1.0 + jax.scipy.special.erf(values * 2.0 ** (-0.5)))
    density = jnp.exp(-0.5 * values * values) * (2.0 * math.pi) ** (-0.5)
    return normal_cdf + values * density


def dot(a, b, ca, cb):
    return lax.dot_general(a, b, (((ca,), (cb,)), ((), ())), preferred_element_type=F32)


def softmax(logits, axis):
    e = jnp.exp(logits - jnp.max(logits, axis=axis, keepdims=True))
    return e / jnp.sum(e, axis=axis, keepdims=True)


def front_kernel(
    tok_hbm, router_hbm, cot_hbm, sg_hbm, logits_hbm, router, tok, cot, sg, logits_ref, combine, rows, in_sems, l_sem, o_sems
):
    images = tok.shape[0]
    half_tiles, total, _ = rows.shape
    experts = router.shape[1]
    stride = total // experts
    pairs = ((router_hbm, router), (tok_hbm, tok), (cot_hbm, cot))
    router_copy, tok_copy, cot_copy = [
        pltpu.make_async_copy(src, dst, in_sems.at[i]) for i, (src, dst) in enumerate(pairs)
    ]
    for copy in (router_copy, tok_copy, cot_copy):
        copy.start()
    router_copy.wait()
    tok_copy.wait()
    for b in range(images):
        logits = dot(tok[b], router[...], 1, 0)
        logits_ref[b] = logits
        combine[b] = softmax(logits, 1).astype(BF)
    sent = [pltpu.make_async_copy(logits_ref, logits_hbm, l_sem)]
    sent[0].start()
    cot_copy.wait()
    for b in range(images):
        slot_grad = dot(combine[b], cot[b], 0, 0)
        for t in range(2 * half_tiles):
            h, j = divmod(t, half_tiles)
            rows[j, pl.ds(2 * b + h, experts, stride), :] = slot_grad[:, t * LANES : (t + 1) * LANES]
    for j in range(half_tiles):
        sg[:, j * LANES : (j + 1) * LANES] = rows[j].astype(BF)
        cols = pl.ds(j * LANES, LANES)
        sent.append(pltpu.make_async_copy(sg.at[:, cols], sg_hbm.at[:, cols], o_sems.at[j]))
        sent[-1].start()
    for copy in sent:
        copy.wait()


def front(tokens, router, cotangent):
    images, m, d = tokens.shape
    experts = router.shape[1]
    total = experts * images * 2
    half_tiles = d // 2 // LANES
    raw = pl.BlockSpec(memory_space=pl.ANY)
    return pl.pallas_call(
        front_kernel,
        in_specs=[raw] * 3,
        out_specs=[raw] * 2,
        out_shape=[
            pltpu.HBM((total, d // 2), BF),
            pltpu.HBM((images, m, experts), F32),
        ],
        scratch_shapes=[
            pltpu.VMEM(router.shape, BF),
            pltpu.VMEM(tokens.shape, BF),
            pltpu.VMEM(tokens.shape, BF),
            pltpu.VMEM((total, d // 2), BF),
            pltpu.VMEM((images, m, experts), F32),
            pltpu.VMEM((images, m, experts), BF),
            pltpu.VMEM((half_tiles, total, LANES), F32),
            pltpu.SemaphoreType.DMA((3,)),
            pltpu.SemaphoreType.DMA(()),
            pltpu.SemaphoreType.DMA((half_tiles,)),
        ],
        compiler_params=pltpu.CompilerParams(vmem_limit_bytes=32 * MIB),
        cost_estimate=cost(4 * images * m * d * experts, 4 * images * m * d + 4 * total * d),
        name="front",
    )(hbm(tokens), hbm(router), hbm(cotangent))


def routing_kernel(logits_ref, cot_ref, out_ref, disp_ref, fc_ref):
    logits = logits_ref[0]
    disp_ref[0] = softmax(logits, 0)
    combine = softmax(logits, 1)
    grad = dot(cot_ref[0], out_ref[0], 1, 1)
    fc_ref[0] = combine * (grad - jnp.sum(combine * grad, axis=1, keepdims=True))


def routing(logits, cotangent, slot_out):
    images, m, experts = logits.shape
    d = cotangent.shape[2]
    small = pl.BlockSpec((1, m, experts), lambda b: (b, 0, 0))
    return pl.pallas_call(
        routing_kernel,
        grid=(images,),
        in_specs=[
            small,
            pl.BlockSpec((1, m, d), lambda b: (b, 0, 0)),
            pl.BlockSpec((1, experts, d), lambda b: (b, 0, 0)),
        ],
        out_specs=[small, small],
        out_shape=[pltpu.HBM(logits.shape, F32)] * 2,
        compiler_params=pltpu.CompilerParams(vmem_limit_bytes=32 * MIB),
        cost_estimate=cost(2 * images * m * d * experts, 2 * (cotangent.size + slot_out.size) + 12 * logits.size),
        name="routing",
    )(hbm(logits), hbm(cotangent), hbm(slot_out))


UP_CUTS = (0, 1024, 2560)
BACK_CUTS = (0, 1280)
WINDOW = 2


def spans(cuts, size):
    return [(lo * size // cuts[-1], hi * size // cuts[-1]) for lo, hi in zip(cuts, cuts[1:])]


def expert_kernel(x_ref, wo_hbm, wi_hbm, slope_hbm, out, wo, wi, slope, wide, rows_ref, pg_ref, w_sems, slope_sems):
    half_tiles, total, _ = wide.shape
    count = total // 2
    ff, d = wo.shape
    ups, backs = spans(UP_CUTS, ff), spans(BACK_CUTS, d)
    groups = []
    for i, (lo, hi) in enumerate(ups):
        cut = pl.ds(lo, hi - lo)
        groups.append([
            pltpu.make_async_copy(wo_hbm.at[cut], wo.at[cut], w_sems.at[i]),
            pltpu.make_async_copy(slope_hbm.at[:, cut], slope.at[:, cut], slope_sems.at[i]),
        ])
    for i, (lo, hi) in enumerate(backs):
        cut = pl.ds(lo, hi - lo)
        groups.append([pltpu.make_async_copy(wi_hbm.at[cut], wi.at[cut], w_sems.at[len(ups) + i])])

    def start(i):
        for copy in groups[i]:
            copy.start()

    def arrive(i):
        for copy in groups[i]:
            copy.wait()
        if i + WINDOW < len(groups):
            start(i + WINDOW)

    for i in range(WINDOW):
        start(i)
    for j in range(half_tiles):
        wide[j] = x_ref[:, j * LANES : (j + 1) * LANES].astype(F32)
    for t in range(2 * half_tiles):
        h, j = divmod(t, half_tiles)
        rows_ref[:, t * LANES : (t + 1) * LANES] = wide[j, pl.ds(h, count, 2), :].astype(BF)
    for i, (lo, hi) in enumerate(ups):
        arrive(i)
        hidden = dot(rows_ref[...], wo[lo:hi, :], 1, 1)
        pg_ref[:, lo:hi] = (hidden * slope[:, lo:hi]).astype(BF)
    done = set()
    for i, (lo, hi) in enumerate(backs):
        arrive(len(ups) + i)
        for t in range(lo // LANES, hi // LANES):
            h, j = divmod(t, half_tiles)
            at = j * LANES
            if j == 0:
                back = dot(pg_ref[...], wi[t * LANES : t * LANES + d // 2, :], 1, 1)
            wide[j, pl.ds(h, count, 2), :] = back[:, at : at + LANES]
            done.add(t)
            if {j, j + half_tiles} <= done:
                cols = slice(j * LANES, (j + 1) * LANES)
                out[:, cols] = wide[j].astype(BF)


def expert(x, w_out, w_in, slope):
    total, half = x.shape
    ff, d = w_out.shape
    raw = pl.BlockSpec(memory_space=pl.ANY)
    return pl.pallas_call(
        expert_kernel,
        in_specs=[WHOLE, raw, raw, raw],
        out_specs=WHOLE,
        out_shape=pltpu.VMEM((total, half), BF),
        scratch_shapes=[
            pltpu.VMEM((ff, d), BF),
            pltpu.VMEM((d, ff), BF),
            pltpu.VMEM(slope.shape, slope.dtype),
            pltpu.VMEM((half // LANES, total, LANES), F32),
            pltpu.VMEM((total // 2, d), BF),
            pltpu.VMEM((total // 2, ff), BF),
            pltpu.SemaphoreType.DMA((len(UP_CUTS) + len(BACK_CUTS) - 2,)),
            pltpu.SemaphoreType.DMA((len(UP_CUTS) - 1,)),
        ],
        compiler_params=pltpu.CompilerParams(vmem_limit_bytes=56 * MIB),
        cost_estimate=cost(2 * total * d * ff, 4 * ff * d + 2 * total * ff),
        name="expert",
    )(vmem(x), hbm(w_out), hbm(w_in), hbm(slope))


def back_kernel(
    y_ref, tok_hbm, disp_hbm, fc_hbm, lg_ref, sb_hbm, term_ref, wide, tok, disp, fc, sb, lg_t, in_sems, out_sems
):
    half_tiles, total, _ = wide.shape
    images, experts, d = sb.shape
    m = tok.shape[1]
    stride = total // experts
    pairs = ((tok_hbm, tok), (disp_hbm, disp), (fc_hbm, fc))
    arrivals = [pltpu.make_async_copy(src, dst, in_sems.at[i]) for i, (src, dst) in enumerate(pairs)]
    for copy in arrivals:
        copy.start()
    for j in range(half_tiles):
        wide[j] = y_ref[:, j * LANES : (j + 1) * LANES].astype(F32)
    for b in range(images):
        for t in range(2 * half_tiles):
            h, j = divmod(t, half_tiles)
            sb[b, :, t * LANES : (t + 1) * LANES] = wide[j, pl.ds(2 * b + h, experts, stride), :].astype(BF)
    for copy in arrivals:
        copy.wait()
    sb_copy = pltpu.make_async_copy(sb, sb_hbm, out_sems.at[0])
    sb_copy.start()
    for b in range(images):
        grad = dot(tok[b], sb[b], 1, 1)
        from_dispatch = disp[b] * (grad - jnp.sum(disp[b] * grad, axis=0, keepdims=True))
        logit_grad = fc[b] + from_dispatch
        lg_ref[b] = logit_grad.astype(BF)
        lg_t[:, b * m : (b + 1) * m] = logit_grad.T.astype(BF)
    term = dot(lg_t[...], tok[...].reshape(images * m, d), 1, 0)
    for h in range(2):
        term_ref[:, h, :] = term[:, h * (d // 2) : (h + 1) * (d // 2)].astype(BF)
    sb_copy.wait()


def back(y, tokens, dispatch, from_combine):
    images, m, d = tokens.shape
    experts = dispatch.shape[2]
    total, half = y.shape
    raw = pl.BlockSpec(memory_space=pl.ANY)
    return pl.pallas_call(
        back_kernel,
        in_specs=[WHOLE, raw, raw, raw],
        out_specs=[WHOLE, raw, WHOLE],
        out_shape=[
            pltpu.VMEM((images, m, experts), BF),
            pltpu.HBM((images, experts, d), BF),
            pltpu.VMEM((experts, 2, d // 2), BF),
        ],
        scratch_shapes=[
            pltpu.VMEM((half // LANES, total, LANES), F32),
            pltpu.VMEM((images, m, d), BF),
            pltpu.VMEM((images, m, experts), F32),
            pltpu.VMEM((images, m, experts), F32),
            pltpu.VMEM((images, experts, d), BF),
            pltpu.VMEM((experts, images * m), BF),
            pltpu.SemaphoreType.DMA((3,)),
            pltpu.SemaphoreType.DMA((1,)),
        ],
        compiler_params=pltpu.CompilerParams(vmem_limit_bytes=32 * MIB),
        cost_estimate=cost(4 * images * m * d * experts, 4 * images * m * d),
        name="back",
    )(vmem(y), hbm(tokens), hbm(dispatch), hbm(from_combine))


def token_kernel(disp_ref, lg_ref, sb_ref, router_t_ref, out_ref):
    b = pl.program_id(0)
    left = jnp.concatenate([disp_ref[0].astype(BF), lg_ref[b]], axis=1)
    right = jnp.concatenate([sb_ref[0], router_t_ref[...]], axis=0)
    out_ref[0] = dot(left, right, 1, 0).astype(BF)


def token_side(dispatch, logit_grad, slot_back, router_t):
    images, m, experts = dispatch.shape
    d = router_t.shape[1]
    return pl.pallas_call(
        token_kernel,
        grid=(images,),
        in_specs=[
            pl.BlockSpec((1, m, experts), lambda b: (b, 0, 0)),
            WHOLE,
            pl.BlockSpec((1, experts, d), lambda b: (b, 0, 0)),
            WHOLE,
        ],
        out_specs=pl.BlockSpec((1, m, d), lambda b: (b, 0, 0)),
        out_shape=pltpu.HBM((images, m, d), BF),
        compiler_params=pltpu.CompilerParams(vmem_limit_bytes=24 * MIB),
        cost_estimate=cost(4 * images * m * d * experts, 4 * images * m * d),
        name="token_side",
    )(hbm(dispatch), vmem(logit_grad), hbm(slot_back), vmem(router_t))


def sum_kernel(scale, x_ref, out_ref):
    step = 8
    part = x_ref[:step].astype(F32)
    for i in range(step, x_ref.shape[0], step):
        part = part + x_ref[i : i + step].astype(F32)
    total = jnp.sum(part, axis=0, keepdims=True) * scale
    out_ref[...] = jnp.broadcast_to(total.astype(BF), out_ref.shape)


def sum_terms(x, scale):
    return pl.pallas_call(
        functools.partial(sum_kernel, scale),
        in_specs=[WHOLE],
        out_specs=WHOLE,
        out_shape=pltpu.HBM(x.shape, BF),
        compiler_params=pltpu.CompilerParams(vmem_limit_bytes=24 * MIB),
        cost_estimate=cost(x.size, 4 * x.size),
        name="sum_terms",
    )(vmem(x))


def finish_kernel(x_ref, out_hbm, out_ref, sems):
    half = x_ref.shape[2]
    wide = x_ref[...].astype(F32)
    sent = []
    for h in range(2):
        part = wide[:, h, :]
        for t in range(half // LANES):
            row = h * half + t * LANES
            out_ref[row : row + LANES, :] = part[:, t * LANES : (t + 1) * LANES].T
        rows = pl.ds(h * half, half)
        sent.append(pltpu.make_async_copy(out_ref.at[rows], out_hbm.at[rows], sems.at[h]))
        sent[-1].start()
    for copy in sent:
        copy.wait()


def finish(x):
    experts, two, half = x.shape
    return pl.pallas_call(
        finish_kernel,
        in_specs=[WHOLE],
        out_specs=pl.BlockSpec(memory_space=pl.ANY),
        out_shape=pltpu.HBM((two * half, experts), F32),
        scratch_shapes=[pltpu.VMEM((two * half, experts), F32), pltpu.SemaphoreType.DMA((2,))],
        compiler_params=pltpu.CompilerParams(vmem_limit_bytes=24 * MIB),
        cost_estimate=cost(x.size, 6 * x.size),
        name="finish",
    )(vmem(x))


def exchange(x):
    return lax.all_to_all(x, AXES, split_axis=0, concat_axis=0, tiled=True)


def exchange_rows(x, devices):
    rows, cols = x.shape
    return exchange(x.reshape(devices, rows // devices, cols)).reshape(rows, cols)


def local(tokens, router, cotangent, slot_out, pre_act, w_in, w_out):
    img_dev = tokens.shape[0]
    devices = lax.axis_size("dp") * lax.axis_size("expert")
    slot_grad, logits = front(tokens, router, cotangent)
    arrived = exchange_rows(slot_grad, devices)

    slope = gelu_slope(pre_act[0].astype(F32))
    dispatch, from_combine = routing(logits, cotangent, slot_out)
    slope, dispatch, from_combine = lax.optimization_barrier((slope, dispatch, from_combine))

    slot_back = expert(arrived, w_out[0], w_in[0], slope)
    returned = exchange_rows(slot_back, devices)
    logit_grad, slot_back, term = back(returned, tokens, dispatch, from_combine)
    terms = exchange(term)
    token_grad = token_side(dispatch, logit_grad, slot_back, router.T)
    gathered = exchange(sum_terms(terms, 1.0 / (img_dev * devices)))
    return token_grad, finish(gathered)


def solution(mesh):
    spec = P(AXES, None, None)
    return jax.shard_map(
        local,
        mesh=mesh,
        in_specs=(spec, P(), spec, spec, spec, spec, spec),
        out_specs=(spec, P()),
        check_vma=False,
    )
```

```python
import functools
import math

import jax
import jax.numpy as jnp
from jax import lax
from jax.experimental import pallas as pl
from jax.experimental.pallas import tpu as pltpu
from jax.sharding import PartitionSpec as P

AXES = ("dp", "expert")
BF = jnp.bfloat16
F32 = jnp.float32
LANES = 128
MIB = 1 << 20


def cost(flops, nbytes, trans=0):
    return pl.CostEstimate(flops=flops, bytes_accessed=nbytes, transcendentals=trans)


def hbm(x):
    return pltpu.with_memory_space_constraint(x, pltpu.HBM)


def vmem(x):
    return pltpu.with_memory_space_constraint(x, pltpu.VMEM)


WHOLE = pl.BlockSpec(memory_space=pltpu.VMEM)


def gelu_slope(values):
    normal_cdf = 0.5 * (1.0 + jax.scipy.special.erf(values * 2.0 ** (-0.5)))
    density = jnp.exp(-0.5 * values * values) * (2.0 * math.pi) ** (-0.5)
    return normal_cdf + values * density


def dot(a, b, ca, cb):
    return lax.dot_general(a, b, (((ca,), (cb,)), ((), ())), preferred_element_type=F32)


def softmax(logits, axis):
    e = jnp.exp(logits - jnp.max(logits, axis=axis, keepdims=True))
    return e / jnp.sum(e, axis=axis, keepdims=True)


def front_kernel(
    tok_hbm, router_hbm, cot_hbm, sg_hbm, logits_hbm, router, tok, cot, sg, logits_ref, combine, rows, in_sems, l_sem, o_sems
):
    images = tok.shape[0]
    half_tiles, total, _ = rows.shape
    experts = router.shape[1]
    stride = total // experts
    pairs = ((router_hbm, router), (tok_hbm, tok), (cot_hbm, cot))
    router_copy, tok_copy, cot_copy = [
        pltpu.make_async_copy(src, dst, in_sems.at[i]) for i, (src, dst) in enumerate(pairs)
    ]
    for copy in (router_copy, tok_copy, cot_copy):
        copy.start()
    router_copy.wait()
    tok_copy.wait()
    for b in range(images):
        logits = dot(tok[b], router[...], 1, 0)
        logits_ref[b] = logits
        combine[b] = softmax(logits, 1).astype(BF)
    sent = [pltpu.make_async_copy(logits_ref, logits_hbm, l_sem)]
    sent[0].start()
    cot_copy.wait()
    for b in range(images):
        slot_grad = dot(combine[b], cot[b], 0, 0)
        for t in range(2 * half_tiles):
            h, j = divmod(t, half_tiles)
            rows[j, pl.ds(2 * b + h, experts, stride), :] = slot_grad[:, t * LANES : (t + 1) * LANES]
    for j in range(half_tiles):
        sg[:, j * LANES : (j + 1) * LANES] = rows[j].astype(BF)
        cols = pl.ds(j * LANES, LANES)
        sent.append(pltpu.make_async_copy(sg.at[:, cols], sg_hbm.at[:, cols], o_sems.at[j]))
        sent[-1].start()
    for copy in sent:
        copy.wait()


def front(tokens, router, cotangent):
    images, m, d = tokens.shape
    experts = router.shape[1]
    total = experts * images * 2
    half_tiles = d // 2 // LANES
    raw = pl.BlockSpec(memory_space=pl.ANY)
    return pl.pallas_call(
        front_kernel,
        in_specs=[raw] * 3,
        out_specs=[raw] * 2,
        out_shape=[
            pltpu.HBM((total, d // 2), BF),
            pltpu.HBM((images, m, experts), F32),
        ],
        scratch_shapes=[
            pltpu.VMEM(router.shape, BF),
            pltpu.VMEM(tokens.shape, BF),
            pltpu.VMEM(tokens.shape, BF),
            pltpu.VMEM((total, d // 2), BF),
            pltpu.VMEM((images, m, experts), F32),
            pltpu.VMEM((images, m, experts), BF),
            pltpu.VMEM((half_tiles, total, LANES), F32),
            pltpu.SemaphoreType.DMA((3,)),
            pltpu.SemaphoreType.DMA(()),
            pltpu.SemaphoreType.DMA((half_tiles,)),
        ],
        compiler_params=pltpu.CompilerParams(vmem_limit_bytes=32 * MIB),
        cost_estimate=cost(4 * images * m * d * experts, 4 * images * m * d + 4 * total * d),
        name="front",
    )(hbm(tokens), hbm(router), hbm(cotangent))


def routing_kernel(logits_ref, cot_ref, out_ref, disp_ref, fc_ref):
    logits = logits_ref[0]
    disp_ref[0] = softmax(logits, 0)
    combine = softmax(logits, 1)
    grad = dot(cot_ref[0], out_ref[0], 1, 1)
    fc_ref[0] = combine * (grad - jnp.sum(combine * grad, axis=1, keepdims=True))


def routing(logits, cotangent, slot_out):
    images, m, experts = logits.shape
    d = cotangent.shape[2]
    small = pl.BlockSpec((1, m, experts), lambda b: (b, 0, 0))
    return pl.pallas_call(
        routing_kernel,
        grid=(images,),
        in_specs=[
            small,
            pl.BlockSpec((1, m, d), lambda b: (b, 0, 0)),
            pl.BlockSpec((1, experts, d), lambda b: (b, 0, 0)),
        ],
        out_specs=[small, small],
        out_shape=[pltpu.HBM(logits.shape, F32)] * 2,
        compiler_params=pltpu.CompilerParams(vmem_limit_bytes=32 * MIB),
        cost_estimate=cost(2 * images * m * d * experts, 2 * (cotangent.size + slot_out.size) + 12 * logits.size),
        name="routing",
    )(hbm(logits), hbm(cotangent), hbm(slot_out))


UP_CUTS = (0, 640, 1536, 2560)
BACK_CUTS = (0, 1280)
WINDOW = 2


def spans(cuts, size):
    return [(lo * size // cuts[-1], hi * size // cuts[-1]) for lo, hi in zip(cuts, cuts[1:])]


def expert_kernel(x_ref, wo_hbm, wi_hbm, slope_hbm, out, wo, wi, slope, wide, rows_ref, pg_ref, w_sems, slope_sems):
    half_tiles, total, _ = wide.shape
    count = total // 2
    ff, d = wo.shape
    ups, backs = spans(UP_CUTS, ff), spans(BACK_CUTS, d)
    groups = []
    for i, (lo, hi) in enumerate(ups):
        cut = pl.ds(lo, hi - lo)
        groups.append([
            pltpu.make_async_copy(wo_hbm.at[cut], wo.at[cut], w_sems.at[i]),
            pltpu.make_async_copy(slope_hbm.at[:, cut], slope.at[:, cut], slope_sems.at[i]),
        ])
    for i, (lo, hi) in enumerate(backs):
        cut = pl.ds(lo, hi - lo)
        groups.append([pltpu.make_async_copy(wi_hbm.at[cut], wi.at[cut], w_sems.at[len(ups) + i])])

    def start(i):
        for copy in groups[i]:
            copy.start()

    def arrive(i):
        for copy in groups[i]:
            copy.wait()
        if i + WINDOW < len(groups):
            start(i + WINDOW)

    start(0)
    for j in range(half_tiles):
        wide[j] = x_ref[:, j * LANES : (j + 1) * LANES].astype(F32)
    for t in range(2 * half_tiles):
        h, j = divmod(t, half_tiles)
        rows_ref[:, t * LANES : (t + 1) * LANES] = wide[j, pl.ds(h, count, 2), :].astype(BF)
    for i in range(1, WINDOW):
        start(i)
    for i, (lo, hi) in enumerate(ups):
        arrive(i)
        hidden = dot(rows_ref[...], wo[lo:hi, :], 1, 1)
        pg_ref[:, lo:hi] = (hidden * slope[:, lo:hi]).astype(BF)
    done = set()
    for i, (lo, hi) in enumerate(backs):
        arrive(len(ups) + i)
        for t in range(lo // LANES, hi // LANES):
            h, j = divmod(t, half_tiles)
            at = j * LANES
            if j == 0:
                back = dot(pg_ref[...], wi[t * LANES : t * LANES + d // 2, :], 1, 1)
            wide[j, pl.ds(h, count, 2), :] = back[:, at : at + LANES]
            done.add(t)
            if {j, j + half_tiles} <= done:
                cols = slice(j * LANES, (j + 1) * LANES)
                out[:, cols] = wide[j].astype(BF)


def expert(x, w_out, w_in, slope):
    total, half = x.shape
    ff, d = w_out.shape
    raw = pl.BlockSpec(memory_space=pl.ANY)
    return pl.pallas_call(
        expert_kernel,
        in_specs=[WHOLE, raw, raw, raw],
        out_specs=WHOLE,
        out_shape=pltpu.VMEM((total, half), BF),
        scratch_shapes=[
            pltpu.VMEM((ff, d), BF),
            pltpu.VMEM((d, ff), BF),
            pltpu.VMEM(slope.shape, slope.dtype),
            pltpu.VMEM((half // LANES, total, LANES), F32),
            pltpu.VMEM((total // 2, d), BF),
            pltpu.VMEM((total // 2, ff), BF),
            pltpu.SemaphoreType.DMA((len(UP_CUTS) + len(BACK_CUTS) - 2,)),
            pltpu.SemaphoreType.DMA((len(UP_CUTS) - 1,)),
        ],
        compiler_params=pltpu.CompilerParams(vmem_limit_bytes=56 * MIB),
        cost_estimate=cost(2 * total * d * ff, 4 * ff * d + 2 * total * ff),
        name="expert",
    )(vmem(x), hbm(w_out), hbm(w_in), hbm(slope))


def back_kernel(
    y_ref, tok_hbm, disp_hbm, fc_hbm, lg_ref, sb_hbm, term_ref, wide, tok, disp, fc, sb, lg_t, in_sems, out_sems
):
    half_tiles, total, _ = wide.shape
    images, experts, d = sb.shape
    m = tok.shape[1]
    stride = total // experts
    pairs = ((tok_hbm, tok), (disp_hbm, disp), (fc_hbm, fc))
    cut = images // 2
    pairs = [(src.at[p], dst.at[p]) for p in (pl.ds(0, cut), pl.ds(cut, images - cut)) for src, dst in pairs]
    arrivals = [pltpu.make_async_copy(src, dst, in_sems.at[i]) for i, (src, dst) in enumerate(pairs)]
    for copy in arrivals:
        copy.start()
    for j in range(half_tiles):
        wide[j] = y_ref[:, j * LANES : (j + 1) * LANES].astype(F32)
    for b in range(images):
        for t in range(2 * half_tiles):
            h, j = divmod(t, half_tiles)
            sb[b, :, t * LANES : (t + 1) * LANES] = wide[j, pl.ds(2 * b + h, experts, stride), :].astype(BF)
    for copy in arrivals[:3]:
        copy.wait()
    sb_copy = pltpu.make_async_copy(sb, sb_hbm, out_sems.at[0])
    sb_copy.start()
    for b in range(images):
        if b == cut:
            for copy in arrivals[3:]:
                copy.wait()
        grad = dot(tok[b], sb[b], 1, 1)
        from_dispatch = disp[b] * (grad - jnp.sum(disp[b] * grad, axis=0, keepdims=True))
        logit_grad = fc[b] + from_dispatch
        lg_ref[b] = logit_grad.astype(BF)
        lg_t[:, b * m : (b + 1) * m] = logit_grad.T.astype(BF)
    term = dot(lg_t[...], tok[...].reshape(images * m, d), 1, 0)
    for h in range(2):
        term_ref[:, h, :] = term[:, h * (d // 2) : (h + 1) * (d // 2)].astype(BF)
    sb_copy.wait()


def back(y, tokens, dispatch, from_combine):
    images, m, d = tokens.shape
    experts = dispatch.shape[2]
    total, half = y.shape
    raw = pl.BlockSpec(memory_space=pl.ANY)
    return pl.pallas_call(
        back_kernel,
        in_specs=[WHOLE, raw, raw, raw],
        out_specs=[WHOLE, raw, WHOLE],
        out_shape=[
            pltpu.VMEM((images, m, experts), BF),
            pltpu.HBM((images, experts, d), BF),
            pltpu.VMEM((experts, 2, d // 2), BF),
        ],
        scratch_shapes=[
            pltpu.VMEM((half // LANES, total, LANES), F32),
            pltpu.VMEM((images, m, d), BF),
            pltpu.VMEM((images, m, experts), F32),
            pltpu.VMEM((images, m, experts), F32),
            pltpu.VMEM((images, experts, d), BF),
            pltpu.VMEM((experts, images * m), BF),
            pltpu.SemaphoreType.DMA((6,)),
            pltpu.SemaphoreType.DMA((1,)),
        ],
        compiler_params=pltpu.CompilerParams(vmem_limit_bytes=32 * MIB),
        cost_estimate=cost(4 * images * m * d * experts, 4 * images * m * d),
        name="back",
    )(vmem(y), hbm(tokens), hbm(dispatch), hbm(from_combine))


def token_kernel(disp_ref, lg_ref, sb_ref, router_t_ref, out_ref):
    b = pl.program_id(0)
    left = jnp.concatenate([disp_ref[0].astype(BF), lg_ref[b]], axis=1)
    right = jnp.concatenate([sb_ref[0], router_t_ref[...]], axis=0)
    out_ref[0] = dot(left, right, 1, 0).astype(BF)


def token_side(dispatch, logit_grad, slot_back, router_t):
    images, m, experts = dispatch.shape
    d = router_t.shape[1]
    return pl.pallas_call(
        token_kernel,
        grid=(images,),
        in_specs=[
            pl.BlockSpec((1, m, experts), lambda b: (b, 0, 0)),
            WHOLE,
            pl.BlockSpec((1, experts, d), lambda b: (b, 0, 0)),
            WHOLE,
        ],
        out_specs=pl.BlockSpec((1, m, d), lambda b: (b, 0, 0)),
        out_shape=pltpu.HBM((images, m, d), BF),
        compiler_params=pltpu.CompilerParams(vmem_limit_bytes=24 * MIB),
        cost_estimate=cost(4 * images * m * d * experts, 4 * images * m * d),
        name="token_side",
    )(hbm(dispatch), vmem(logit_grad), hbm(slot_back), vmem(router_t))


def sum_kernel(scale, x_ref, out_ref):
    step = 8
    part = x_ref[:step].astype(F32)
    for i in range(step, x_ref.shape[0], step):
        part = part + x_ref[i : i + step].astype(F32)
    total = jnp.sum(part, axis=0, keepdims=True) * scale
    out_ref[...] = jnp.broadcast_to(total.astype(BF), out_ref.shape)


def sum_terms(x, scale):
    return pl.pallas_call(
        functools.partial(sum_kernel, scale),
        in_specs=[WHOLE],
        out_specs=WHOLE,
        out_shape=pltpu.HBM(x.shape, BF),
        compiler_params=pltpu.CompilerParams(vmem_limit_bytes=24 * MIB),
        cost_estimate=cost(x.size, 4 * x.size),
        name="sum_terms",
    )(vmem(x))


def finish_kernel(x_ref, out_hbm, out_ref, sems):
    half = x_ref.shape[2]
    wide = x_ref[...].astype(F32)
    sent = []
    for h in range(2):
        part = wide[:, h, :]
        for t in range(half // LANES):
            row = h * half + t * LANES
            out_ref[row : row + LANES, :] = part[:, t * LANES : (t + 1) * LANES].T
        rows = pl.ds(h * half, half)
        sent.append(pltpu.make_async_copy(out_ref.at[rows], out_hbm.at[rows], sems.at[h]))
        sent[-1].start()
    for copy in sent:
        copy.wait()


def finish(x):
    experts, two, half = x.shape
    return pl.pallas_call(
        finish_kernel,
        in_specs=[WHOLE],
        out_specs=pl.BlockSpec(memory_space=pl.ANY),
        out_shape=pltpu.HBM((two * half, experts), F32),
        scratch_shapes=[pltpu.VMEM((two * half, experts), F32), pltpu.SemaphoreType.DMA((2,))],
        compiler_params=pltpu.CompilerParams(vmem_limit_bytes=24 * MIB),
        cost_estimate=cost(x.size, 6 * x.size),
        name="finish",
    )(vmem(x))


def exchange(x):
    return lax.all_to_all(x, AXES, split_axis=0, concat_axis=0, tiled=True)


def exchange_rows(x, devices):
    rows, cols = x.shape
    return exchange(x.reshape(devices, rows // devices, cols)).reshape(rows, cols)


def local(tokens, router, cotangent, slot_out, pre_act, w_in, w_out):
    img_dev = tokens.shape[0]
    devices = lax.axis_size("dp") * lax.axis_size("expert")
    slot_grad, logits = front(tokens, router, cotangent)
    arrived = exchange_rows(slot_grad, devices)

    slope = gelu_slope(pre_act[0].astype(F32))
    dispatch, from_combine = routing(logits, cotangent, slot_out)
    slope, dispatch, from_combine = lax.optimization_barrier((slope, dispatch, from_combine))

    slot_back = expert(arrived, w_out[0], w_in[0], slope)
    returned = exchange_rows(slot_back, devices)
    logit_grad, slot_back, term = back(returned, tokens, dispatch, from_combine)
    terms = exchange(term)
    token_grad = token_side(dispatch, logit_grad, slot_back, router.T)
    gathered = exchange(sum_terms(terms, 1.0 / (img_dev * devices)))
    return token_grad, finish(gathered)


def solution(mesh):
    spec = P(AXES, None, None)
    return jax.shard_map(
        local,
        mesh=mesh,
        in_specs=(spec, P(), spec, spec, spec, spec, spec),
        out_specs=(spec, P()),
        check_vma=False,
    )
```
